32 devices in a mesh: dp: 16 (over z, y, core), tensor: 2 (over x).
Axes of the slice: x: 2, y: 2, z: 4, core: 2. Of those that a mesh axis runs over, the one named last changes fastest.
Arguments:
- hidden: bfloat16 [4096, 1024], P(('dp', 'tensor')), may hold values from -6 to 6
- cotangent: bfloat16 [4096, 1024], P(('dp', 'tensor')), may hold values from -6 to 6
- lengths: int32 [16], P('dp'), may hold values from 129 to 256, as said below
- norm_gain: float32 [1024], replicated, may hold values from 0.1 to 1.9
- w_gate: bfloat16 [1024, 2048], P('dp', 'tensor'), may hold values from -0.1875 to 0.1875
- w_x: bfloat16 [1024, 2048], P('dp', 'tensor'), may hold values from -0.1875 to 0.1875
- w_bc: bfloat16 [1024, 256], P('dp'), may hold values from -0.1875 to 0.1875
- w_dt: bfloat16 [1024, 32], P('dp', 'tensor'), may hold values from -0.1875 to 0.1875
- conv_x: float32 [4, 2048], P(None, 'tensor'), may hold values from -3 to 3
- conv_x_bias: float32 [2048], P('tensor'), may hold values from -3 to 3
- conv_bc: float32 [4, 256], replicated, may hold values from -3 to 3
- conv_bc_bias: float32 [256], replicated, may hold values from -3 to 3
- dt_bias: float32 [32], P('tensor'), may hold values from -6 to -2
- a_log: float32 [32], P('tensor'), may hold values from 0 to 2.77
- d_skip: float32 [32], P('tensor'), may hold values from 0.5 to 2
- gated_gain: float32 [2048], P('tensor'), may hold values from 0.1 to 1.9
- w_out: bfloat16 [2048, 1024], P('tensor', 'dp'), may hold values from -0.125 to 0.125
Outputs:
- output: bfloat16 [4096, 1024], P(('dp', 'tensor'))
- d_hidden: bfloat16 [4096, 1024], P(('dp', 'tensor'))
- g_norm_gain: float32 [1024], replicated
- g_w_gate: float32 [1024, 2048], P('dp', 'tensor')
- g_w_x: float32 [1024, 2048], P('dp', 'tensor')
- g_w_bc: float32 [1024, 256], P('dp')
- g_w_dt: float32 [1024, 32], P('dp', 'tensor')
- g_conv_x: float32 [4, 2048], P(None, 'tensor')
- g_conv_x_bias: float32 [2048], P('tensor')
- g_conv_bc: float32 [4, 256], replicated
- g_conv_bc_bias: float32 [256], replicated
- g_dt_bias: float32 [32], P('tensor')
- g_a_log: float32 [32], P('tensor')
- g_d_skip: float32 [32], P('tensor')
- g_gated_gain: float32 [2048], P('tensor')
- g_w_out: float32 [2048, 1024], P('tensor', 'dp')
The draws below stay inside these ranges and needn't reach their ends.
Inputs may be any that keep to these rules, and one draw needn't show every extreme that they name: The tokens of data group g fill its first lengths[g] slots; in every draw some group's length is exactly 256.
All inputs are finite; a program needn't handle non-finite values.
Results may differ from the reference program's by a relative error of at most 0.0085.
Values may be sent and summed in bfloat16 or wider, within the bound.
A program may use at most 128 MiB of HBM per device.

```python
import jax
import jax.numpy as jnp
from jax import lax

D = 1024
HEADS = 32
HEAD_DIM = 64
STATE = 128
CONV = 4
SPAN = 256
SEQ_LEN = 256
DI = 2048
TOKENS = 4096


def draw_lengths(key, part):
    key = jax.random.fold_in(key, 7)
    key_lengths, key_longest = jax.random.split(key)
    groups = TOKENS // SEQ_LEN
    drawn_lengths = jax.random.randint(key_lengths, (groups,), SEQ_LEN // 2 + 1, SEQ_LEN + 1)
    longest = jax.random.randint(key_longest, (), 0, groups)
    return jnp.where(jnp.arange(groups) == longest, SEQ_LEN, drawn_lengths).astype(jnp.int32)


def levels(own_key, dims, pieces, low, high):
    def one(dim, parts):
        draws = jax.random.uniform(jax.random.fold_in(jax.random.fold_in(own_key, 6), dim), (parts,), jnp.float32, low / len(pieces), high / len(pieces))
        return jnp.repeat(jnp.exp(draws), dims[dim] // parts).reshape((-1,) + (1,) * (len(dims) - dim - 1))

    loudness = one(*pieces[0])
    for cut in pieces[1:]:
        loudness = loudness * one(*cut)
    return loudness


def bell_draw(own_key, dims, scale, reach, pieces=(), kind=jnp.bfloat16):
    entries = jax.random.normal(own_key, dims, jnp.float32) * scale
    if len(pieces) > 0:
        entries = levels(own_key, dims, pieces, -0.22, 0.18) * entries
    return jnp.clip(entries, min=-reach, max=reach).astype(kind)


def setup_inputs(seed: int = 0) -> dict:
    key_of = jax.random.split(jax.random.key(seed), 18)
    return {
        "hidden": bell_draw(key_of[0], (TOKENS, D), 1.0, 6.0, ((0, 32),)),
        "cotangent": bell_draw(key_of[1], (TOKENS, D), 1.0, 6.0, ((0, 32),)),
        "lengths": draw_lengths(jax.random.fold_in(key_of[17], 71), 0),
        "norm_gain": jnp.clip(1.0 + 0.18 * jax.random.normal(key_of[3], (D,), jnp.float32), 0.1, 1.9),
        "w_gate": bell_draw(key_of[4], (D, DI), D ** -0.5, 0.1875, ((0, 16), (1, 2))),
        "w_x": bell_draw(key_of[5], (D, DI), D ** -0.5, 0.1875, ((0, 16), (1, 2))),
        "w_bc": bell_draw(key_of[6], (D, 2 * STATE), D ** -0.5, 0.1875, ((0, 16),)),
        "w_dt": bell_draw(key_of[7], (D, HEADS), D ** -0.5, 0.1875, ((0, 16), (1, 2))),
        "conv_x": bell_draw(key_of[8], (CONV, DI), CONV ** -0.5, 3.0, ((1, 2),), jnp.float32),
        "conv_x_bias": bell_draw(key_of[9], (DI,), 0.5, 3.0, ((0, 2),), jnp.float32),
        "conv_bc": bell_draw(key_of[10], (CONV, 2 * STATE), CONV ** -0.5, 3.0, (), jnp.float32),
        "conv_bc_bias": bell_draw(key_of[11], (2 * STATE,), 0.5, 3.0, (), jnp.float32),
        "dt_bias": jnp.clip(-6.0 + 4.0 * jax.random.uniform(key_of[12], (HEADS,), jnp.float32) ** levels(key_of[12], (HEADS,), ((0, 2),), -0.2, 0.2), -6.0, -2.0),
        "a_log": jnp.clip(2.77 * jax.random.uniform(key_of[13], (HEADS,), jnp.float32) ** levels(key_of[13], (HEADS,), ((0, 2),), -0.2, 0.2), 0.0, 2.77),
        "d_skip": jnp.clip(0.5 + 1.5 * jax.random.uniform(key_of[14], (HEADS,), jnp.float32) ** levels(key_of[14], (HEADS,), ((0, 2),), -0.2, 0.2), 0.5, 2.0),
        "gated_gain": jnp.clip(1.0 + 0.18 * jax.random.normal(key_of[15], (DI,), jnp.float32), 0.1, 1.9),
        "w_out": bell_draw(key_of[16], (DI, D), DI ** -0.5, 0.125, ((0, 2), (1, 16))),
    }


EPSILON = 1e-05
HIGHEST = lax.Precision.HIGHEST

@jax.custom_vjp
def low(v):
    return lax.optimization_barrier(v.astype(jnp.bfloat16)).astype(jnp.float32)

@jax.custom_vjp
def low_back(v):
    return v

def low_keep(v):
    return (low(v), None)

def low_pass(kept, grad):
    return (grad,)

def back_keep(v):
    return (v, None)

def back_low(kept, grad):
    return (low(grad),)
low.defvjp(low_keep, low_pass)
low_back.defvjp(back_keep, back_low)

def causal_conv(values, kernel, offsets):
    taps_count = kernel.shape[0]
    length_rows = values.shape[0]
    padded = jnp.concatenate([jnp.zeros((taps_count - 1, values.shape[1]), values.dtype), values], axis=0)
    summed = offsets[None, :] + jnp.zeros_like(values)
    for tap_index in range(taps_count):
        summed = summed + kernel[tap_index][None, :] * padded[tap_index:tap_index + length_rows]
    return summed

def span_scan(x_heads, dt_heads, decay_rates, b_mat, c_mat, block_len):
    seq_len, n_heads, head_dim = x_heads.shape
    n_blocks = seq_len // block_len
    x_blocks = x_heads.reshape(n_blocks, block_len, n_heads, head_dim)
    dt_blocks = dt_heads.reshape(n_blocks, block_len, n_heads)
    b_blocks = b_mat.reshape(n_blocks, block_len, -1)
    c_blocks = c_mat.reshape(n_blocks, block_len, -1)
    log_decay = jnp.cumsum(dt_blocks * decay_rates[None, None, :], axis=1)
    weighted = x_blocks * dt_blocks[..., None]
    positions = jnp.arange(block_len)
    causal = (positions[:, None] >= positions[None, :])[None, None]
    log_heads = jnp.swapaxes(log_decay, 1, 2)
    decay_gaps = log_heads[:, :, :, None] - log_heads[:, :, None, :]
    decays = jnp.where(causal, jnp.exp(jnp.where(causal, decay_gaps, 0.0)), 0.0)
    intersection = jnp.einsum('cqn,csn->cqs', c_blocks, b_blocks, precision=HIGHEST)
    mixing = intersection[:, None] * decays
    y_inner = jnp.einsum('chqs,cshp->cqhp', mixing, weighted, precision=HIGHEST)
    to_end = jnp.exp(log_decay[:, -1:, :] - log_decay)
    states = jnp.einsum('csn,cshp->chnp', b_blocks, weighted * to_end[..., None], precision=HIGHEST)
    block_decay = jnp.exp(log_decay[:, -1, :])

    def carry_step(carried, inputs):
        new_state, factor = inputs
        return (carried * factor[:, None, None] + new_state, carried)
    start_state = jnp.zeros(states.shape[1:], states.dtype)
    final_state, entering = lax.scan(carry_step, start_state, (states, block_decay))
    y_outer = jnp.einsum('cqn,chnp,cqh->cqhp', c_blocks, entering, jnp.exp(log_decay), precision=HIGHEST)
    return (y_inner + y_outer).reshape(seq_len, n_heads, head_dim)

def mix_bc(bc_raw, conv_bc, conv_bc_bias):
    return jax.nn.silu(causal_conv(bc_raw, conv_bc, conv_bc_bias))

def mixer(x_raw, bc_vals, dt_raw, conv_x, conv_x_bias, dt_bias, a_log, d_skip):
    x_conv = jax.nn.silu(causal_conv(x_raw, conv_x, conv_x_bias))
    n_heads = dt_raw.shape[1]
    x_heads = x_conv.reshape(x_raw.shape[0], n_heads, HEAD_DIM)
    dt_vals = jax.nn.softplus(dt_raw + dt_bias[None, :])
    decay_rates = -jnp.exp(a_log)
    y_heads = span_scan(x_heads, dt_vals, decay_rates, bc_vals[:, :STATE], bc_vals[:, STATE:], SPAN)
    y_heads = y_heads + d_skip[None, :, None] * x_heads
    return y_heads.reshape(x_raw.shape[0], -1)

def branch(h_seq, m_seq, params):
    norm_gain, w_gate, w_x, w_bc, w_dt, conv_x, conv_x_bias, conv_bc, conv_bc_bias, dt_bias, a_log, d_skip, gated_gain, w_out = params
    row_scale = lax.rsqrt(lax.optimization_barrier(jnp.mean(h_seq * h_seq, axis=1, keepdims=True)) + EPSILON)
    normed = low(h_seq * row_scale * norm_gain[None, :])
    gate_raw = low_back(jnp.dot(normed, w_gate, precision=HIGHEST))
    x_raw = low_back(jnp.dot(normed, w_x, precision=HIGHEST))
    bc_raw = low_back(jnp.dot(normed, w_bc, precision=HIGHEST))
    dt_raw = low_back(jnp.dot(normed, w_dt, precision=HIGHEST))
    bc_vals = mix_bc(bc_raw, conv_bc, conv_bc_bias)
    mixer_out = mixer(x_raw, bc_vals, dt_raw, conv_x, conv_x_bias, dt_bias, a_log, d_skip)
    gated_vals = mixer_out * jax.nn.silu(gate_raw)
    gate_scale = lax.rsqrt(lax.optimization_barrier(jnp.mean(gated_vals * gated_vals, axis=1, keepdims=True)) + EPSILON)
    normed_y = low(gated_vals * gate_scale * gated_gain[None, :])
    branch_out = low_back(jnp.dot(normed_y, w_out, precision=HIGHEST))
    return m_seq[:, None] * branch_out

def widen(array):
    return array.astype(jnp.float32)

def reference(hidden, cotangent, lengths, norm_gain, w_gate, w_x, w_bc, w_dt, conv_x, conv_x_bias, conv_bc, conv_bc_bias, dt_bias, a_log, d_skip, gated_gain, w_out):
    groups = lengths.shape[0]
    hidden_vals = hidden.astype(jnp.float32).reshape(groups, SEQ_LEN, D)
    cot_vals = cotangent.astype(jnp.float32).reshape(groups, SEQ_LEN, D)
    positions = jnp.arange(SEQ_LEN, dtype=jnp.int32)
    live_mask = (positions[None, :] < lengths.astype(jnp.int32)[:, None]).astype(jnp.float32)
    params = tuple(map(widen, (norm_gain, w_gate, w_x, w_bc, w_dt, conv_x, conv_x_bias, conv_bc, conv_bc_bias, dt_bias, a_log, d_skip, gated_gain, w_out)))

    def forward(h_all, param_set):

        def one_seq(seq_pair):
            return branch(seq_pair[0], seq_pair[1], param_set)
        branches = lax.map(jax.checkpoint(one_seq), (h_all, live_mask))
        return h_all + branches
    out_vals, pullback = jax.vjp(forward, hidden_vals, params)
    grad_hidden, grads = pullback(cot_vals)
    return (out_vals.reshape(groups * SEQ_LEN, D).astype(jnp.bfloat16), grad_hidden.reshape(groups * SEQ_LEN, D).astype(jnp.bfloat16), grads[0], grads[1], grads[2], grads[3], grads[4], grads[5], grads[6], grads[7], grads[8], grads[9], grads[10], grads[11], grads[12], grads[13])
```

```python
import functools

import jax
import jax.numpy as jnp
from jax import lax
from jax.experimental import pallas as pl
from jax.experimental.pallas import tpu as pltpu
from jax.sharding import PartitionSpec as P

HEADS = 32
HEAD_DIM = 64
STATE = 128
SPAN = 256
LANES = 128
MESH = pl.DeviceIdType.MESH

EPSILON = 1e-05
HIGHEST = lax.Precision.HIGHEST


def chip_at(pos, chips):
    pos = lax.rem(pos + 4 * chips, chips)
    up = (pos < chips // 2).astype(jnp.int32)
    return up * (2 * pos) + (1 - up) * (2 * (chips - 1 - pos) + 1)


def place_of(chip, chips):
    odd = lax.rem(chip, 2)
    return (1 - odd) * (chip // 2) + odd * (chips - 1 - chip // 2)


def gather_kernel(
    chips, wg, wx, wo, wb, nrm, grd, og, ox, oo, ob, on, ogr,
    ring_send, ring_recv, sib_send, sib_recv, ten_send, ten_recv, loc_sem,
):
    me = lax.axis_index("dp")
    rank = lax.axis_index("tensor")
    core = lax.rem(me, 2)
    chip = me // 2
    way = 1 - 2 * core
    pos = place_of(chip, chips)
    right = 2 * chip_at(pos + way, chips) + core
    left = 2 * chip_at(pos - way, chips) + core
    sibling = 2 * chip + 1 - core
    other = 1 - rank
    barrier = pltpu.get_barrier_semaphore()
    for target in ((right, rank), (left, rank), (sibling, rank), (me, other)):
        pl.semaphore_signal(barrier, inc=1, device_id=target, device_id_type=MESH)
    pl.semaphore_wait(barrier, 4)
    ins = (wg, wx, wo, wb)
    outs = (og, ox, oo, ob)

    def owned(step, which_core):
        turn = 1 - 2 * which_core
        return 2 * chip_at(pos - step * turn, chips) + which_core

    def ring(step, piece, arriving=False):
        slot = owned(step + 1 if arriving else step, core)
        dst = outs[piece].at[slot]
        src = ins[piece] if (step == 0 and not arriving) else dst
        return pltpu.make_async_remote_copy(
            src_ref=src, dst_ref=dst, send_sem=ring_send.at[step, piece],
            recv_sem=ring_recv.at[step, piece], device_id=(right, rank), device_id_type=MESH,
        )

    def side(step, piece, arriving=False):
        slot = owned(step, 1 - core if arriving else core)
        dst = outs[piece].at[slot]
        src = ins[piece] if (step == 0 and not arriving) else dst
        return pltpu.make_async_remote_copy(
            src_ref=src, dst_ref=dst, send_sem=sib_send.at[step, piece],
            recv_sem=sib_recv.at[step, piece], device_id=(sibling, rank), device_id_type=MESH,
        )

    def over(which, arriving=False):
        slot = other if arriving else rank
        src = (nrm, grd)[which]
        return pltpu.make_async_remote_copy(
            src_ref=src, dst_ref=(on, ogr)[which].at[slot], send_sem=ten_send.at[which],
            recv_sem=ten_recv.at[which], device_id=(me, other), device_id_type=MESH,
        )

    for piece in range(4):
        ring(0, piece).start()
    for which in range(2):
        over(which).start()
    for piece in range(4):
        side(0, piece).start()
    local = [pltpu.make_async_copy(ins[p], outs[p].at[me], loc_sem.at[p]) for p in range(4)]
    local += [
        pltpu.make_async_copy((nrm, grd)[w], (on, ogr)[w].at[rank], loc_sem.at[4 + w])
        for w in range(2)
    ]
    for copy in local:
        copy.start()
    for step in range(1, chips):
        for piece in range(4):
            ring(step - 1, piece, True).wait_recv()
            if step < chips - 1:
                ring(step, piece).start()
            side(step, piece).start()
    for copy in local:
        copy.wait()
    for which in range(2):
        over(which).wait_send()
        over(which, True).wait_recv()
    for step in range(chips):
        for piece in range(4):
            if step < chips - 1:
                ring(step, piece).wait_send()
            side(step, piece).wait_send()
            side(step, piece, True).wait_recv()


def gather_all(wg, wx, wo, wb, nrm, grd):
    count = lax.axis_size("dp")
    chips = count // 2
    anywhere = pl.BlockSpec(memory_space=pl.ANY)
    dma = pltpu.SemaphoreType.DMA
    outs = [jax.ShapeDtypeStruct((count,) + a.shape, a.dtype) for a in (wg, wx, wo, wb)]
    outs += [jax.ShapeDtypeStruct((2,) + a.shape, a.dtype) for a in (nrm, grd)]
    res = pl.pallas_call(
        functools.partial(gather_kernel, chips),
        out_shape=outs,
        in_specs=[anywhere] * 6,
        out_specs=[anywhere] * 6,
        scratch_shapes=[
            dma((chips - 1, 4)), dma((chips - 1, 4)), dma((chips, 4)), dma((chips, 4)),
            dma((2,)), dma((2,)), dma((6,)),
        ],
        compiler_params=pltpu.CompilerParams(collective_id=0, has_side_effects=True),
        name="gather_weights",
    )(wg, wx, wo, wb, nrm, grd)
    return [r.reshape(r.shape[0] * r.shape[1], r.shape[2]) for r in res]


def reduce_kernel(
    chips, stages, gg, gx, go, gb, small, og, ox, oo, ob, osmall,
    sg, sx, so, sb, tg, tx, to, tb, rg, rx, ro, rb, acc, got,
    sib_send, sib_recv, ring_send, ring_recv, fly_send, fly_recv,
):
    me = lax.axis_index("dp")
    rank = lax.axis_index("tensor")
    core = lax.rem(me, 2)
    chip = me // 2
    way = 1 - 2 * core
    pos = place_of(chip, chips)
    right = 2 * chip_at(pos + way, chips) + core
    left = 2 * chip_at(pos - way, chips) + core
    sibling = 2 * chip + 1 - core
    other = 1 - rank

    def partner(stage):
        if stage == stages:
            return (me, other)
        bit = 1 << stage
        return (me + bit - 2 * bit * lax.rem(me // bit, 2), rank)

    barrier = pltpu.get_barrier_semaphore()
    targets = [(right, rank), (left, rank)] + [partner(s) for s in range(stages + 1)]
    for target in targets:
        pl.semaphore_signal(barrier, inc=1, device_id=target, device_id_type=MESH)
    pl.semaphore_wait(barrier, len(targets))
    ins = (gg, gx, go, gb)
    sibs = (sg, sx, so, sb)
    sends = (tg, tx, to, tb)
    gots = (rg, rx, ro, rb)
    outs = (og, ox, oo, ob)

    def target_chip(step, which_core):
        turn = 1 - 2 * which_core
        return chip_at(pos - turn * (1 + step), chips)

    def side(step, piece):
        src = ins[piece].at[2 * target_chip(step, 1 - core) + 1 - core]
        return pltpu.make_async_remote_copy(
            src_ref=src, dst_ref=sibs[piece].at[step], send_sem=sib_send.at[step, piece],
            recv_sem=sib_recv.at[step, piece], device_id=(sibling, rank), device_id_type=MESH,
        )

    def ring(step, piece):
        return pltpu.make_async_remote_copy(
            src_ref=sends[piece].at[step], dst_ref=gots[piece].at[step],
            send_sem=ring_send.at[step, piece], recv_sem=ring_recv.at[step, piece],
            device_id=(right, rank), device_id_type=MESH,
        )

    def fly(stage):
        rows = pl.ds(8, 8) if stage == stages else pl.ds(0, 16)
        return pltpu.make_async_remote_copy(
            src_ref=acc.at[stage, rows], dst_ref=got.at[stage, rows],
            send_sem=fly_send.at[stage], recv_sem=fly_recv.at[stage],
            device_id=partner(stage), device_id_type=MESH,
        )

    def fly_end(stage):
        fly(stage).wait_recv()
        if stage == stages:
            osmall[pl.ds(0, 8), :] = acc[stage, pl.ds(0, 8), :]
            osmall[pl.ds(8, 8), :] = acc[stage, pl.ds(8, 8), :] + got[stage, pl.ds(8, 8), :]
        else:
            acc[stage + 1] = acc[stage] + got[stage]

    for step in range(chips):
        for piece in range(4):
            side(step, piece).start()
    acc[0] = small[...]
    fly(0).start()
    for step in range(chips):
        own = 2 * target_chip(step, core) + core
        for piece in range(4):
            side(step, piece).wait_recv()
            total = ins[piece][own].astype(jnp.float32) + sibs[piece][step].astype(jnp.float32)
            if step > 0:
                ring(step - 1, piece).wait_recv()
                total = total + gots[piece][step - 1].astype(jnp.float32)
            if step < chips - 1:
                sends[piece][step] = total.astype(jnp.bfloat16)
                ring(step, piece).start()
            else:
                outs[piece][...] = total
        if step <= stages:
            fly_end(step)
            if step < stages:
                fly(step + 1).start()
    for stage in range(chips, stages + 1):
        fly_end(stage)
        if stage < stages:
            fly(stage + 1).start()
    for step in range(chips):
        for piece in range(4):
            side(step, piece).wait_send()
            if step < chips - 1:
                ring(step, piece).wait_send()
    for stage in range(stages + 1):
        fly(stage).wait_send()


def reduce_all(gg, gx, go, gb, small):
    count = lax.axis_size("dp")
    chips = count // 2
    stages = count.bit_length() - 1
    vmem = pl.BlockSpec(memory_space=pltpu.VMEM)
    dma = pltpu.SemaphoreType.DMA
    parts = [g.reshape(count, g.shape[0] // count, g.shape[1]) for g in (gg, gx, go, gb)]
    outs = [jax.ShapeDtypeStruct(p.shape[1:], jnp.float32) for p in parts]
    outs.append(jax.ShapeDtypeStruct(small.shape, jnp.float32))
    bufs = [pltpu.VMEM((chips,) + p.shape[1:], jnp.bfloat16) for p in parts]
    slots = [pltpu.VMEM((chips - 1,) + p.shape[1:], jnp.bfloat16) for p in parts]
    return pl.pallas_call(
        functools.partial(reduce_kernel, chips, stages),
        out_shape=outs,
        in_specs=[vmem] * 5,
        out_specs=[vmem] * 5,
        scratch_shapes=bufs + slots + slots + [
            pltpu.VMEM((stages + 1,) + small.shape, jnp.float32),
            pltpu.VMEM((stages + 1,) + small.shape, jnp.float32),
            dma((chips, 4)), dma((chips, 4)), dma((chips - 1, 4)), dma((chips - 1, 4)),
            dma((stages + 1,)), dma((stages + 1,)),
        ],
        compiler_params=pltpu.CompilerParams(
            collective_id=1, has_side_effects=True, vmem_limit_bytes=50 * 1024 * 1024
        ),
        name="reduce_grads",
    )(*parts, small)


def swap(values):
    return lax.ppermute(values, "tensor", [(0, 1), (1, 0)])


def pair_sum(values):
    return values + swap(values)


def pair_scatter(values, rank):
    rows = values.shape[0] // 2
    halves = values.reshape(2, rows, values.shape[1])
    mine = lax.dynamic_index_in_dim(halves, rank, 0, keepdims=False)
    theirs = lax.dynamic_index_in_dim(halves, 1 - rank, 0, keepdims=False)
    return mine + swap(theirs.astype(jnp.bfloat16)).astype(jnp.float32)


def causal_conv(values, kernel, offsets):
    taps_count = kernel.shape[0]
    length_rows = values.shape[0]
    padded = jnp.concatenate(
        [jnp.zeros((taps_count - 1, values.shape[1]), values.dtype), values], axis=0
    )
    summed = offsets[None, :] + jnp.zeros_like(values)
    for tap_index in range(taps_count):
        summed = summed + kernel[tap_index][None, :] * padded[tap_index : tap_index + length_rows]
    return summed


def span_scan(x_heads, dt_heads, decay_rates, b_mat, c_mat, block_len):
    seq_len, n_heads, head_dim = x_heads.shape
    n_blocks = seq_len // block_len
    x_blocks = x_heads.reshape(n_blocks, block_len, n_heads, head_dim)
    dt_blocks = dt_heads.reshape(n_blocks, block_len, n_heads)
    b_blocks = b_mat.reshape(n_blocks, block_len, -1)
    c_blocks = c_mat.reshape(n_blocks, block_len, -1)
    log_decay = jnp.cumsum(dt_blocks * decay_rates[None, None, :], axis=1)
    weighted = x_blocks * dt_blocks[..., None]
    positions = jnp.arange(block_len)
    causal = (positions[:, None] >= positions[None, :])[None, None]
    log_heads = jnp.swapaxes(log_decay, 1, 2)
    decay_gaps = log_heads[:, :, :, None] - log_heads[:, :, None, :]
    decays = jnp.where(causal, jnp.exp(jnp.where(causal, decay_gaps, 0.0)), 0.0)
    intersection = jnp.einsum("cqn,csn->cqs", c_blocks, b_blocks, precision=HIGHEST)
    mixing = intersection[:, None] * decays
    y_inner = jnp.einsum("chqs,cshp->cqhp", mixing, weighted, precision=HIGHEST)
    return y_inner.reshape(seq_len, n_heads, head_dim)


def mix_bc(bc_raw, conv_bc, conv_bc_bias):
    return jax.nn.silu(causal_conv(bc_raw, conv_bc, conv_bc_bias))


def mixer(x_raw, bc_vals, dt_raw, conv_x, conv_x_bias, dt_bias, a_log, d_skip):
    x_conv = jax.nn.silu(causal_conv(x_raw, conv_x, conv_x_bias))
    n_heads = dt_raw.shape[1]
    x_heads = x_conv.reshape(x_raw.shape[0], n_heads, HEAD_DIM)
    dt_vals = jax.nn.softplus(dt_raw + dt_bias[None, :])
    decay_rates = -jnp.exp(a_log)
    y_heads = span_scan(x_heads, dt_vals, decay_rates, bc_vals[:, :STATE], bc_vals[:, STATE:], SPAN)
    y_heads = y_heads + d_skip[None, :, None] * x_heads
    return y_heads.reshape(x_raw.shape[0], -1)


def times_right(left, right):
    return jnp.dot(left, right, preferred_element_type=jnp.float32)


def times_back(left, right):
    return lax.dot_general(
        left, right, (((1,), (1,)), ((), ())), preferred_element_type=jnp.float32
    )


def over_rows(left, right):
    return lax.dot_general(
        left, right, (((0,), (0,)), ((), ())), preferred_element_type=jnp.float32
    )


def body(
    hidden,
    cotangent,
    lengths,
    norm_gain,
    w_gate,
    w_x,
    w_bc,
    w_dt,
    conv_x,
    conv_x_bias,
    conv_bc,
    conv_bc_bias,
    dt_bias,
    a_log,
    d_skip,
    gated_gain,
    w_out,
):
    own_rows, model_width = hidden.shape
    rank = lax.axis_index("tensor")
    inner_width = HEADS * HEAD_DIM
    bc_cols = w_bc.shape[1]
    dt_cols = w_dt.shape[1]
    fill = -(bc_cols + dt_cols) % LANES
    hidden_vals = hidden.astype(jnp.float32)
    row_scale = lax.rsqrt(jnp.mean(hidden_vals * hidden_vals, axis=1, keepdims=True) + EPSILON)
    normed_own = (hidden_vals * row_scale * norm_gain[None, :]).astype(jnp.bfloat16)
    positions = rank * own_rows + jnp.arange(own_rows, dtype=jnp.int32)
    live_rows = (positions < lengths[0]).astype(jnp.float32)[:, None]
    cot_vals = cotangent.astype(jnp.float32)
    grad_branch = (live_rows * cot_vals).astype(jnp.bfloat16)
    w_small = jnp.concatenate([w_bc, w_dt, jnp.zeros((w_bc.shape[0], fill), w_bc.dtype)], axis=1)
    full_gate, full_x, full_out, full_small, normed, grad_full = gather_all(
        w_gate, w_x, w_out.T, w_small, normed_own, grad_branch
    )
    gate_raw = times_right(normed, full_gate)
    x_raw = times_right(normed, full_x)
    small_raw = times_right(normed, full_small)
    bc_raw = small_raw[:, :bc_cols]
    dt_raw = small_raw[:, bc_cols : bc_cols + dt_cols]
    bc_vals, bc_pull = jax.vjp(mix_bc, bc_raw, conv_bc, conv_bc_bias)
    mixer_out, mix_pull = jax.vjp(
        mixer, x_raw, bc_vals, dt_raw, conv_x, conv_x_bias, dt_bias, a_log, d_skip
    )
    gate_act = jax.nn.silu(gate_raw)
    gated_vals = mixer_out * gate_act
    grad_y = times_right(grad_full, full_out)
    weighted_grad = grad_y * gated_gain[None, :]
    row_sums = pair_sum(
        jnp.stack(
            [jnp.sum(gated_vals * gated_vals, axis=1), jnp.sum(gated_vals * weighted_grad, axis=1)]
        )
    )
    gate_scale = lax.rsqrt(row_sums[0] / inner_width + EPSILON)[:, None]
    cross_sum = row_sums[1]
    normed_y = (gated_vals * gate_scale * gated_gain[None, :]).astype(jnp.bfloat16)
    branch_own = pair_scatter(times_back(normed_y, full_out), rank)
    output = (hidden_vals + live_rows * branch_own).astype(jnp.bfloat16)
    grad_w_out = over_rows(grad_full, normed_y).astype(jnp.bfloat16)
    grad_gated_gain = jnp.sum(grad_y * gated_vals * gate_scale, axis=0)
    grad_gated = (
        gate_scale * weighted_grad - gated_vals * gate_scale**3 * (cross_sum / inner_width)[:, None]
    )
    gate_sigmoid = jax.nn.sigmoid(gate_raw)
    grad_mixer = grad_gated * gate_act
    grad_gate = (
        grad_gated * mixer_out * gate_sigmoid * (1.0 + gate_raw * (1.0 - gate_sigmoid))
    ).astype(jnp.bfloat16)
    (
        grad_x_f,
        grad_bc_part,
        grad_dt_f,
        grad_conv_x,
        grad_conv_x_bias,
        grad_dt_bias,
        grad_a_log,
        grad_d_skip,
    ) = mix_pull(grad_mixer)
    grad_bc_f, grad_conv_bc, grad_conv_bc_bias = bc_pull(pair_sum(grad_bc_part))
    grad_x = grad_x_f.astype(jnp.bfloat16)
    grad_bc = grad_bc_f.astype(jnp.bfloat16)
    grad_dt = grad_dt_f.astype(jnp.bfloat16)
    tail = jnp.zeros((grad_dt.shape[0], fill), jnp.bfloat16)
    grad_small = jnp.concatenate([grad_bc, grad_dt, tail], axis=1)
    first = (rank == 0).astype(jnp.bfloat16)
    grad_kept = jnp.concatenate([grad_bc * first, grad_dt, tail], axis=1)
    g_gate = over_rows(normed, grad_gate).astype(jnp.bfloat16)
    g_x = over_rows(normed, grad_x).astype(jnp.bfloat16)
    g_small = over_rows(normed, grad_small).astype(jnp.bfloat16)
    grad_normed = (
        times_back(grad_gate, full_gate)
        + times_back(grad_x, full_x)
        + times_back(grad_kept, full_small)
    )
    grad_normed_own = pair_scatter(grad_normed, rank)
    grad_norm_part = jnp.sum(hidden_vals * row_scale * grad_normed_own, axis=0)
    weighted_in = grad_normed_own * norm_gain[None, :]
    inner_sum = jnp.sum(hidden_vals * weighted_in, axis=1, keepdims=True)
    grad_hidden = row_scale * weighted_in - hidden_vals * row_scale**3 * inner_sum / model_width
    d_hidden = (cot_vals + grad_hidden).astype(jnp.bfloat16)
    heads = grad_dt_bias.shape[0]
    taps = conv_x.shape[0]
    mixed = jnp.concatenate([grad_conv_bc_bias, grad_dt_bias, grad_a_log, grad_d_skip])
    small = jnp.concatenate(
        [
            grad_conv_x,
            grad_conv_x_bias[None],
            grad_gated_gain[None],
            grad_conv_bc.reshape(1, -1),
            jnp.pad(mixed, (0, model_width - mixed.shape[0]))[None],
            grad_norm_part[None],
            jnp.zeros((7, model_width), jnp.float32),
        ],
        axis=0,
    )
    sum_gate, sum_x, sum_out, sum_small, summed = reduce_all(g_gate, g_x, grad_w_out, g_small, small)
    rest = summed[taps + 3]
    return (
        output,
        d_hidden,
        summed[8],
        sum_gate,
        sum_x,
        sum_small[:, :bc_cols],
        sum_small[:, bc_cols : bc_cols + dt_cols],
        summed[:taps],
        summed[taps],
        summed[taps + 2].reshape(conv_bc.shape),
        rest[:bc_cols],
        rest[bc_cols : bc_cols + heads],
        rest[bc_cols + heads : bc_cols + 2 * heads],
        rest[bc_cols + 2 * heads : bc_cols + 3 * heads],
        summed[taps + 1],
        sum_out.T,
    )


def solution(mesh):
    placed = (
        P(("dp", "tensor"), None),
        P(("dp", "tensor"), None),
        P("dp"),
        P(),
        P("dp", "tensor"),
        P("dp", "tensor"),
        P("dp", None),
        P("dp", "tensor"),
        P(None, "tensor"),
        P("tensor"),
        P(),
        P(),
        P("tensor"),
        P("tensor"),
        P("tensor"),
        P("tensor"),
        P("tensor", "dp"),
    )
    return jax.shard_map(
        body,
        mesh=mesh,
        in_specs=placed,
        out_specs=(
            P(("dp", "tensor"), None),
            P(("dp", "tensor"), None),
            P(),
            P("dp", "tensor"),
            P("dp", "tensor"),
            P("dp", None),
            P("dp", "tensor"),
            P(None, "tensor"),
            P("tensor"),
            P(),
            P(),
            P("tensor"),
            P("tensor"),
            P("tensor"),
            P("tensor"),
            P("tensor", "dp"),
        ),
        check_vma=False,
    )
```

```python
import functools

import jax
import jax.numpy as jnp
from jax import lax
from jax.experimental import pallas as pl
from jax.experimental.pallas import tpu as pltpu
from jax.sharding import PartitionSpec as P

HEADS = 32
HEAD_DIM = 64
STATE = 128
LANES = 128
MESH = pl.DeviceIdType.MESH

EPSILON = 1e-05
HIGHEST = lax.Precision.HIGHEST


def chip_at(pos, chips):
    pos = lax.rem(pos + 4 * chips, chips)
    up = (pos < chips // 2).astype(jnp.int32)
    return up * (2 * pos) + (1 - up) * (2 * (chips - 1 - pos) + 1)


def place_of(chip, chips):
    odd = lax.rem(chip, 2)
    return (1 - odd) * (chip // 2) + odd * (chips - 1 - chip // 2)


def gather_kernel(
    chips, wg, wx, wo, wb, nrm, grd, og, ox, oo, ob, on, ogr,
    ring_send, ring_recv, sib_send, sib_recv, ten_send, ten_recv, loc_sem,
):
    me = lax.axis_index("dp")
    rank = lax.axis_index("tensor")
    core = lax.rem(me, 2)
    chip = me // 2
    way = 1 - 2 * core
    pos = place_of(chip, chips)
    right = 2 * chip_at(pos + way, chips) + core
    left = 2 * chip_at(pos - way, chips) + core
    sibling = 2 * chip + 1 - core
    other = 1 - rank
    barrier = pltpu.get_barrier_semaphore()
    for target in ((right, rank), (left, rank), (sibling, rank), (me, other)):
        pl.semaphore_signal(barrier, inc=1, device_id=target, device_id_type=MESH)
    pl.semaphore_wait(barrier, 4)
    ins = (wg, wx, wo, wb)
    outs = (og, ox, oo, ob)

    def owned(step, which_core):
        turn = 1 - 2 * which_core
        return 2 * chip_at(pos - step * turn, chips) + which_core

    def ring(step, piece, arriving=False):
        slot = owned(step + 1 if arriving else step, core)
        dst = outs[piece].at[slot]
        src = ins[piece] if (step == 0 and not arriving) else dst
        return pltpu.make_async_remote_copy(
            src_ref=src, dst_ref=dst, send_sem=ring_send.at[step, piece],
            recv_sem=ring_recv.at[step, piece], device_id=(right, rank), device_id_type=MESH,
        )

    def side(step, piece, arriving=False):
        slot = owned(step, 1 - core if arriving else core)
        dst = outs[piece].at[slot]
        src = ins[piece] if (step == 0 and not arriving) else dst
        return pltpu.make_async_remote_copy(
            src_ref=src, dst_ref=dst, send_sem=sib_send.at[step, piece],
            recv_sem=sib_recv.at[step, piece], device_id=(sibling, rank), device_id_type=MESH,
        )

    def over(which, arriving=False):
        slot = other if arriving else rank
        src = (nrm, grd)[which]
        return pltpu.make_async_remote_copy(
            src_ref=src, dst_ref=(on, ogr)[which].at[slot], send_sem=ten_send.at[which],
            recv_sem=ten_recv.at[which], device_id=(me, other), device_id_type=MESH,
        )

    for piece in range(4):
        ring(0, piece).start()
    for which in range(2):
        over(which).start()
    for piece in range(4):
        side(0, piece).start()
    local = [pltpu.make_async_copy(ins[p], outs[p].at[me], loc_sem.at[p]) for p in range(4)]
    local += [
        pltpu.make_async_copy((nrm, grd)[w], (on, ogr)[w].at[rank], loc_sem.at[4 + w])
        for w in range(2)
    ]
    for copy in local:
        copy.start()
    for step in range(1, chips):
        for piece in range(4):
            ring(step - 1, piece, True).wait_recv()
            if step < chips - 1:
                ring(step, piece).start()
            side(step, piece).start()
    for copy in local:
        copy.wait()
    for which in range(2):
        over(which).wait_send()
        over(which, True).wait_recv()
    for step in range(chips):
        for piece in range(4):
            if step < chips - 1:
                ring(step, piece).wait_send()
            side(step, piece).wait_send()
            side(step, piece, True).wait_recv()


def gather_all(wg, wx, wo, wb, nrm, grd):
    count = lax.axis_size("dp")
    chips = count // 2
    anywhere = pl.BlockSpec(memory_space=pl.ANY)
    dma = pltpu.SemaphoreType.DMA
    outs = [jax.ShapeDtypeStruct((count,) + a.shape, a.dtype) for a in (wg, wx, wo, wb)]
    outs += [jax.ShapeDtypeStruct((2,) + a.shape, a.dtype) for a in (nrm, grd)]
    res = pl.pallas_call(
        functools.partial(gather_kernel, chips),
        out_shape=outs,
        in_specs=[anywhere] * 6,
        out_specs=[anywhere] * 6,
        scratch_shapes=[
            dma((chips - 1, 4)), dma((chips - 1, 4)), dma((chips, 4)), dma((chips, 4)),
            dma((2,)), dma((2,)), dma((6,)),
        ],
        compiler_params=pltpu.CompilerParams(collective_id=0, has_side_effects=True),
        name="gather_weights",
    )(wg, wx, wo, wb, nrm, grd)
    return [r.reshape(r.shape[0] * r.shape[1], r.shape[2]) for r in res]


def reduce_kernel(
    chips, stages, gg, gx, go, gb, small, og, ox, oo, ob, osmall,
    sg, sx, so, sb, tg, tx, to, tb, rg, rx, ro, rb, acc, got,
    sib_send, sib_recv, ring_send, ring_recv, fly_send, fly_recv,
):
    me = lax.axis_index("dp")
    rank = lax.axis_index("tensor")
    core = lax.rem(me, 2)
    chip = me // 2
    way = 1 - 2 * core
    pos = place_of(chip, chips)
    right = 2 * chip_at(pos + way, chips) + core
    left = 2 * chip_at(pos - way, chips) + core
    sibling = 2 * chip + 1 - core
    other = 1 - rank

    def partner(stage):
        if stage == stages:
            return (me, other)
        bit = 1 << stage
        return (me + bit - 2 * bit * lax.rem(me // bit, 2), rank)

    barrier = pltpu.get_barrier_semaphore()
    targets = [(right, rank), (left, rank)] + [partner(s) for s in range(stages + 1)]
    for target in targets:
        pl.semaphore_signal(barrier, inc=1, device_id=target, device_id_type=MESH)
    pl.semaphore_wait(barrier, len(targets))
    ins = (gg, gx, go, gb)
    sibs = (sg, sx, so, sb)
    sends = (tg, tx, to, tb)
    gots = (rg, rx, ro, rb)
    outs = (og, ox, oo, ob)

    def target_chip(step, which_core):
        turn = 1 - 2 * which_core
        return chip_at(pos - turn * (1 + step), chips)

    def side(step, piece):
        src = ins[piece].at[2 * target_chip(step, 1 - core) + 1 - core]
        return pltpu.make_async_remote_copy(
            src_ref=src, dst_ref=sibs[piece].at[step], send_sem=sib_send.at[step, piece],
            recv_sem=sib_recv.at[step, piece], device_id=(sibling, rank), device_id_type=MESH,
        )

    def ring(step, piece):
        return pltpu.make_async_remote_copy(
            src_ref=sends[piece].at[step], dst_ref=gots[piece].at[step],
            send_sem=ring_send.at[step, piece], recv_sem=ring_recv.at[step, piece],
            device_id=(right, rank), device_id_type=MESH,
        )

    def fly(stage):
        rows = pl.ds(8, 8) if stage == stages else pl.ds(0, 16)
        return pltpu.make_async_remote_copy(
            src_ref=acc.at[stage, rows], dst_ref=got.at[stage, rows],
            send_sem=fly_send.at[stage], recv_sem=fly_recv.at[stage],
            device_id=partner(stage), device_id_type=MESH,
        )

    def fly_end(stage):
        fly(stage).wait_recv()
        if stage == stages:
            osmall[pl.ds(0, 8), :] = acc[stage, pl.ds(0, 8), :]
            osmall[pl.ds(8, 8), :] = acc[stage, pl.ds(8, 8), :] + got[stage, pl.ds(8, 8), :]
        else:
            acc[stage + 1] = acc[stage] + got[stage]

    for step in range(chips):
        for piece in range(4):
            side(step, piece).start()
    acc[0] = small[...]
    fly(0).start()
    for step in range(chips):
        own = 2 * target_chip(step, core) + core
        for piece in range(4):
            side(step, piece).wait_recv()
            total = ins[piece][own].astype(jnp.float32) + sibs[piece][step].astype(jnp.float32)
            if step > 0:
                ring(step - 1, piece).wait_recv()
                total = total + gots[piece][step - 1].astype(jnp.float32)
            if step < chips - 1:
                sends[piece][step] = total.astype(jnp.bfloat16)
                ring(step, piece).start()
            else:
                outs[piece][...] = total
        if step <= stages:
            fly_end(step)
            if step < stages:
                fly(step + 1).start()
    for stage in range(chips, stages + 1):
        fly_end(stage)
        if stage < stages:
            fly(stage + 1).start()
    for step in range(chips):
        for piece in range(4):
            side(step, piece).wait_send()
            if step < chips - 1:
                ring(step, piece).wait_send()
    for stage in range(stages + 1):
        fly(stage).wait_send()


def reduce_all(gg, gx, go, gb, small):
    count = lax.axis_size("dp")
    chips = count // 2
    stages = count.bit_length() - 1
    vmem = pl.BlockSpec(memory_space=pltpu.VMEM)
    dma = pltpu.SemaphoreType.DMA
    parts = [g.reshape(count, g.shape[0] // count, g.shape[1]) for g in (gg, gx, go, gb)]
    outs = [jax.ShapeDtypeStruct(p.shape[1:], jnp.float32) for p in parts]
    outs.append(jax.ShapeDtypeStruct(small.shape, jnp.float32))
    bufs = [pltpu.VMEM((chips,) + p.shape[1:], jnp.bfloat16) for p in parts]
    slots = [pltpu.VMEM((chips - 1,) + p.shape[1:], jnp.bfloat16) for p in parts]
    return pl.pallas_call(
        functools.partial(reduce_kernel, chips, stages),
        out_shape=outs,
        in_specs=[vmem] * 5,
        out_specs=[vmem] * 5,
        scratch_shapes=bufs + slots + slots + [
            pltpu.VMEM((stages + 1,) + small.shape, jnp.float32),
            pltpu.VMEM((stages + 1,) + small.shape, jnp.float32),
            dma((chips, 4)), dma((chips, 4)), dma((chips - 1, 4)), dma((chips - 1, 4)),
            dma((stages + 1,)), dma((stages + 1,)),
        ],
        compiler_params=pltpu.CompilerParams(
            collective_id=1, has_side_effects=True, vmem_limit_bytes=50 * 1024 * 1024
        ),
        name="reduce_grads",
    )(*parts, small)


def swap(values):
    return lax.ppermute(values, "tensor", [(0, 1), (1, 0)])


def pair_sum(values):
    return values + swap(values)


def pair_scatter(values, rank):
    rows = values.shape[0] // 2
    halves = values.reshape(2, rows, values.shape[1])
    mine = lax.dynamic_index_in_dim(halves, rank, 0, keepdims=False)
    theirs = lax.dynamic_index_in_dim(halves, 1 - rank, 0, keepdims=False)
    return mine + swap(theirs.astype(jnp.bfloat16)).astype(jnp.float32)


def causal_conv(values, kernel, offsets):
    taps_count = kernel.shape[0]
    length_rows = values.shape[0]
    padded = jnp.concatenate(
        [jnp.zeros((taps_count - 1, values.shape[1]), values.dtype), values], axis=0
    )
    summed = offsets[None, :] + jnp.zeros_like(values)
    for tap_index in range(taps_count):
        summed = summed + kernel[tap_index][None, :] * padded[tap_index : tap_index + length_rows]
    return summed


def mix_bc(bc_raw, conv_bc, conv_bc_bias):
    return jax.nn.silu(causal_conv(bc_raw, conv_bc, conv_bc_bias))


ROWS = (((0,), (0,)), ((), ()))
COLS = (((1,), (1,)), ((), ()))
PLAIN = (((1,), (0,)), ((), ()))


def halves_of(values):
    high = values.astype(jnp.bfloat16)
    return high, (values - high.astype(jnp.float32)).astype(jnp.bfloat16)


def split_dot(left, right, dims):
    def one(x, y):
        return lax.dot_general(x, y, dims, preferred_element_type=jnp.float32)

    return one(left[0], right[0]) + (one(left[0], right[1]) + one(left[1], right[0]))


def shifted(values, count, rows):
    if count == 0:
        return values
    size = values.shape[0]
    rolled = pltpu.roll(values, count % size, 0)
    keep = rows >= count if count > 0 else rows < size + count
    return jnp.where(keep, rolled, 0.0)


def pick_column(values, index, lanes):
    return jnp.sum(jnp.where(lanes == index, values, 0.0), axis=1, keepdims=True)


def conv_parts(x_ref, par_ref, rows, taps):
    x_raw = x_ref[...]
    moved = [shifted(x_raw, taps - 1 - j, rows) for j in range(taps)]
    summed = par_ref[pl.ds(taps, 1), :] + jnp.zeros_like(x_raw)
    for j in range(taps):
        summed = summed + par_ref[pl.ds(j, 1), :] * moved[j]
    sig = 1.0 / (1.0 + jnp.exp(-summed))
    return moved, summed, sig


def head_decay(log_ref, log_t_ref, head, lanes, causal):
    column = pick_column(log_ref[...], head, lanes)
    gaps = column - log_t_ref[pl.ds(head, 1), :]
    return jnp.where(causal, jnp.exp(jnp.where(causal, gaps, 0.0)), 0.0)


def scan_setup(bc_ref, cross_ref):
    @pl.when(pl.program_id(0) == 0)
    def _():
        cross_ref[...] = lax.dot_general(
            bc_ref[:, STATE:], bc_ref[:, :STATE], COLS,
            precision=HIGHEST, preferred_element_type=jnp.float32,
        )

    size = cross_ref.shape[0]
    rows = lax.broadcasted_iota(jnp.int32, (size, LANES), 0)
    lanes = lax.broadcasted_iota(jnp.int32, (size, LANES), 1)
    wide_rows = lax.broadcasted_iota(jnp.int32, (size, size), 0)
    wide_cols = lax.broadcasted_iota(jnp.int32, (size, size), 1)
    return rows, lanes, wide_rows, wide_cols


def scan_kernel(taps, x_ref, bc_ref, par_ref, dt_ref, log_ref, log_t_ref, y_ref, cross_ref):
    rows, lanes, wide_rows, wide_cols = scan_setup(bc_ref, cross_ref)
    causal = wide_rows >= wide_cols
    base = 2 * pl.program_id(0)
    left = lanes < HEAD_DIM
    _, summed, sig = conv_parts(x_ref, par_ref, rows, taps)
    x_vals = summed * sig
    dt_all = dt_ref[...]
    dt_pair = jnp.where(
        left, pick_column(dt_all, base, lanes), pick_column(dt_all, base + 1, lanes)
    )
    weighted = halves_of(x_vals * dt_pair)
    parts = []
    for k in range(2):
        mixing = cross_ref[...] * head_decay(log_ref, log_t_ref, base + k, lanes, causal)
        parts.append(split_dot(halves_of(mixing), weighted, PLAIN))
    y_ref[...] = jnp.where(left, parts[0], parts[1]) + par_ref[pl.ds(taps + 1, 1), :] * x_vals


def back_kernel(
    taps, x_ref, bc_ref, par_ref, dt_ref, log_ref, log_t_ref, gy_ref,
    gx_ref, gbc_ref, gpar_ref, gdt_ref, grow_ref, gcol_ref, cross_ref, gcross_ref,
):
    step = pl.program_id(0)

    @pl.when(step == 0)
    def _():
        gcross_ref[...] = jnp.zeros_like(gcross_ref)
        gdt_ref[...] = jnp.zeros_like(gdt_ref)
        grow_ref[...] = jnp.zeros_like(grow_ref)

    rows, lanes, wide_rows, wide_cols = scan_setup(bc_ref, cross_ref)
    causal = wide_rows >= wide_cols
    strict = wide_rows > wide_cols
    base = 2 * step
    left = lanes < HEAD_DIM
    moved, summed, sig = conv_parts(x_ref, par_ref, rows, taps)
    x_vals = summed * sig
    dt_all = dt_ref[...]
    dt_pair = jnp.where(
        left, pick_column(dt_all, base, lanes), pick_column(dt_all, base + 1, lanes)
    )
    weighted = halves_of(x_vals * dt_pair)
    grad_y = gy_ref[...]
    parts = []
    for k in range(2):
        own = left if k == 0 else jnp.logical_not(left)
        grad_own = halves_of(jnp.where(own, grad_y, 0.0))
        decay = head_decay(log_ref, log_t_ref, base + k, lanes, causal)
        grad_decayed = split_dot(grad_own, weighted, COLS) * decay
        gcross_ref[...] += grad_decayed
        mixing = cross_ref[...] * decay
        parts.append(split_dot(halves_of(mixing), grad_own, ROWS))
        flow = jnp.where(strict, grad_decayed * cross_ref[...], 0.0)
        grow_ref[...] += jnp.where(lanes == base + k, jnp.sum(flow, axis=1, keepdims=True), 0.0)
        gcol_ref[pl.ds(base + k, 1), :] = jnp.sum(flow, axis=0, keepdims=True)
    grad_w = parts[0] + parts[1]
    through = grad_w * x_vals
    for k in range(2):
        own = left if k == 0 else jnp.logical_not(left)
        total = jnp.sum(jnp.where(own, through, 0.0), axis=1, keepdims=True)
        gdt_ref[...] += jnp.where(lanes == base + k, total, 0.0)
    grad_x = grad_w * dt_pair + par_ref[pl.ds(taps + 1, 1), :] * grad_y
    grad_sum = grad_x * sig * (1.0 + summed * (1.0 - sig))
    back = jnp.zeros_like(grad_sum)
    for j in range(taps):
        back = back + par_ref[pl.ds(j, 1), :] * shifted(grad_sum, j + 1 - taps, rows)
        gpar_ref[pl.ds(j, 1), :] = jnp.sum(grad_sum * moved[j], axis=0, keepdims=True)
    gpar_ref[pl.ds(taps, 1), :] = jnp.sum(grad_sum, axis=0, keepdims=True)
    gpar_ref[pl.ds(taps + 1, 1), :] = jnp.sum(grad_y * x_vals, axis=0, keepdims=True)
    gpar_ref[pl.ds(taps + 2, 2), :] = jnp.zeros((2, LANES), jnp.float32)
    gx_ref[...] = back.astype(jnp.bfloat16)

    @pl.when(step == pl.num_programs(0) - 1)
    def _():
        pair = gcross_ref[...]
        gbc_ref[:, STATE:] = lax.dot_general(
            pair, bc_ref[:, :STATE], PLAIN, precision=HIGHEST, preferred_element_type=jnp.float32
        )
        gbc_ref[:, :STATE] = lax.dot_general(
            pair, bc_ref[:, STATE:], ROWS, precision=HIGHEST, preferred_element_type=jnp.float32
        )


def mixer_call(taps, backward, x_raw, *args):
    size, width = x_raw.shape
    f32 = jnp.float32
    block = pl.BlockSpec((size, LANES), lambda i: (0, i))
    narrow = pl.BlockSpec((8, LANES), lambda i: (0, i))

    def whole(shape):
        return pl.BlockSpec(shape, lambda i: (0, 0))

    bc_vals, params, dt_pad, log_pad, log_t = args[:5]
    in_specs = [block, whole(bc_vals.shape), narrow] + [whole(a.shape) for a in args[2:5]]
    square = pltpu.VMEM((size, size), f32)
    if backward:
        in_specs.append(block)
        out_shape = [
            jax.ShapeDtypeStruct((size, width), jnp.bfloat16),
            jax.ShapeDtypeStruct(bc_vals.shape, f32),
            jax.ShapeDtypeStruct(params.shape, f32),
            jax.ShapeDtypeStruct(dt_pad.shape, f32),
            jax.ShapeDtypeStruct(dt_pad.shape, f32),
            jax.ShapeDtypeStruct(log_t.shape, f32),
        ]
        out_specs = [block, whole(bc_vals.shape), narrow] + [whole(o.shape) for o in out_shape[3:]]
    else:
        out_shape = jax.ShapeDtypeStruct((size, width), f32)
        out_specs = block
    return pl.pallas_call(
        functools.partial(back_kernel if backward else scan_kernel, taps),
        grid=(width // LANES,),
        out_shape=out_shape,
        in_specs=in_specs,
        out_specs=out_specs,
        scratch_shapes=[square, square] if backward else [square],
        compiler_params=pltpu.CompilerParams(vmem_limit_bytes=40 * 1024 * 1024),
        cost_estimate=pl.CostEstimate(
            flops=(3 if backward else 1) * 6 * size * size * width,
            bytes_accessed=8 * size * width, transcendentals=size * size * width // HEAD_DIM,
        ),
        name="mixer_back" if backward else "mixer_scan",
    )(x_raw, *args)


def times_right(left, right):
    return jnp.dot(left, right, preferred_element_type=jnp.float32)


def times_back(left, right):
    return lax.dot_general(
        left, right, (((1,), (1,)), ((), ())), preferred_element_type=jnp.float32
    )


def over_rows(left, right):
    return lax.dot_general(
        left, right, (((0,), (0,)), ((), ())), preferred_element_type=jnp.float32
    )


def body(
    hidden,
    cotangent,
    lengths,
    norm_gain,
    w_gate,
    w_x,
    w_bc,
    w_dt,
    conv_x,
    conv_x_bias,
    conv_bc,
    conv_bc_bias,
    dt_bias,
    a_log,
    d_skip,
    gated_gain,
    w_out,
):
    own_rows, model_width = hidden.shape
    rank = lax.axis_index("tensor")
    inner_width = HEADS * HEAD_DIM
    bc_cols = w_bc.shape[1]
    dt_cols = w_dt.shape[1]
    fill = -(bc_cols + dt_cols) % LANES
    hidden_vals = hidden.astype(jnp.float32)
    row_scale = lax.rsqrt(jnp.mean(hidden_vals * hidden_vals, axis=1, keepdims=True) + EPSILON)
    normed_own = (hidden_vals * row_scale * norm_gain[None, :]).astype(jnp.bfloat16)
    positions = rank * own_rows + jnp.arange(own_rows, dtype=jnp.int32)
    live_rows = (positions < lengths[0]).astype(jnp.float32)[:, None]
    cot_vals = cotangent.astype(jnp.float32)
    grad_branch = (live_rows * cot_vals).astype(jnp.bfloat16)
    w_small = jnp.concatenate([w_bc, w_dt, jnp.zeros((w_bc.shape[0], fill), w_bc.dtype)], axis=1)
    full_gate, full_x, full_out, full_small, normed, grad_full = gather_all(
        w_gate, w_x, w_out.T, w_small, normed_own, grad_branch
    )
    gate_raw = times_right(normed, full_gate)
    x_raw = times_right(normed, full_x)
    small_raw = times_right(normed, full_small)
    bc_raw = small_raw[:, :bc_cols]
    dt_raw = small_raw[:, bc_cols : bc_cols + dt_cols]
    bc_vals, bc_pull = jax.vjp(mix_bc, bc_raw, conv_bc, conv_bc_bias)
    heads = dt_cols
    taps = conv_x.shape[0]
    dt_in = dt_raw + dt_bias[None, :]
    dt_vals = jax.nn.softplus(dt_in)
    rates = -jnp.exp(a_log)
    size = dt_vals.shape[0]
    lower = jnp.tril(jnp.ones((size, size), jnp.float32))
    log_decay = jnp.dot(lower, dt_vals * rates[None, :], precision=HIGHEST)
    wide = ((0, 0), (0, LANES - heads))
    params = jnp.concatenate(
        [
            conv_x,
            conv_x_bias[None],
            jnp.repeat(d_skip, HEAD_DIM)[None],
            jnp.zeros((2, conv_x.shape[1]), jnp.float32),
        ],
        axis=0,
    )
    mix_args = (bc_vals, params, jnp.pad(dt_vals, wide), jnp.pad(log_decay, wide), log_decay.T)
    mixer_out = mixer_call(taps, False, x_raw, *mix_args)
    gate_act = jax.nn.silu(gate_raw)
    gated_vals = mixer_out * gate_act
    grad_y = times_right(grad_full, full_out)
    weighted_grad = grad_y * gated_gain[None, :]
    row_sums = pair_sum(
        jnp.stack(
            [jnp.sum(gated_vals * gated_vals, axis=1), jnp.sum(gated_vals * weighted_grad, axis=1)]
        )
    )
    gate_scale = lax.rsqrt(row_sums[0] / inner_width + EPSILON)[:, None]
    cross_sum = row_sums[1]
    normed_y = (gated_vals * gate_scale * gated_gain[None, :]).astype(jnp.bfloat16)
    branch_own = pair_scatter(times_back(normed_y, full_out), rank)
    output = (hidden_vals + live_rows * branch_own).astype(jnp.bfloat16)
    grad_w_out = over_rows(grad_full, normed_y).astype(jnp.bfloat16)
    grad_gated_gain = jnp.sum(grad_y * gated_vals * gate_scale, axis=0)
    grad_gated = (
        gate_scale * weighted_grad - gated_vals * gate_scale**3 * (cross_sum / inner_width)[:, None]
    )
    gate_sigmoid = jax.nn.sigmoid(gate_raw)
    grad_mixer = grad_gated * gate_act
    grad_gate = (
        grad_gated * mixer_out * gate_sigmoid * (1.0 + gate_raw * (1.0 - gate_sigmoid))
    ).astype(jnp.bfloat16)
    grad_x, grad_bc_part, grad_params, direct, from_rows, from_cols = mixer_call(
        taps, True, x_raw, *mix_args, grad_mixer
    )
    grad_bc_f, grad_conv_bc, grad_conv_bc_bias = bc_pull(pair_sum(grad_bc_part))
    grad_log = from_rows[:, :heads] - from_cols.T
    grad_step = lax.dot_general(lower, grad_log, ROWS, precision=HIGHEST)
    grad_dt_f = (direct[:, :heads] + grad_step * rates[None, :]) * jax.nn.sigmoid(dt_in)
    grad_dt_bias = jnp.sum(grad_dt_f, axis=0)
    grad_a_log = rates * jnp.sum(grad_step * dt_vals, axis=0)
    grad_conv_x = grad_params[:taps]
    grad_conv_x_bias = grad_params[taps]
    grad_d_skip = jnp.sum(grad_params[taps + 1].reshape(heads, HEAD_DIM), axis=1)
    grad_bc = grad_bc_f.astype(jnp.bfloat16)
    grad_dt = grad_dt_f.astype(jnp.bfloat16)
    tail = jnp.zeros((grad_dt.shape[0], fill), jnp.bfloat16)
    grad_small = jnp.concatenate([grad_bc, grad_dt, tail], axis=1)
    first = (rank == 0).astype(jnp.bfloat16)
    grad_kept = jnp.concatenate([grad_bc * first, grad_dt, tail], axis=1)
    g_gate = over_rows(normed, grad_gate).astype(jnp.bfloat16)
    g_x = over_rows(normed, grad_x).astype(jnp.bfloat16)
    g_small = over_rows(normed, grad_small).astype(jnp.bfloat16)
    grad_normed = (
        times_back(grad_gate, full_gate)
        + times_back(grad_x, full_x)
        + times_back(grad_kept, full_small)
    )
    grad_normed_own = pair_scatter(grad_normed, rank)
    grad_norm_part = jnp.sum(hidden_vals * row_scale * grad_normed_own, axis=0)
    weighted_in = grad_normed_own * norm_gain[None, :]
    inner_sum = jnp.sum(hidden_vals * weighted_in, axis=1, keepdims=True)
    grad_hidden = row_scale * weighted_in - hidden_vals * row_scale**3 * inner_sum / model_width
    d_hidden = (cot_vals + grad_hidden).astype(jnp.bfloat16)
    mixed = jnp.concatenate([grad_conv_bc_bias, grad_dt_bias, grad_a_log, grad_d_skip])
    small = jnp.concatenate(
        [
            grad_conv_x,
            grad_conv_x_bias[None],
            grad_gated_gain[None],
            grad_conv_bc.reshape(1, -1),
            jnp.pad(mixed, (0, model_width - mixed.shape[0]))[None],
            grad_norm_part[None],
            jnp.zeros((7, model_width), jnp.float32),
        ],
        axis=0,
    )
    sum_gate, sum_x, sum_out, sum_small, summed = reduce_all(g_gate, g_x, grad_w_out, g_small, small)
    rest = summed[taps + 3]
    return (
        output,
        d_hidden,
        summed[8],
        sum_gate,
        sum_x,
        sum_small[:, :bc_cols],
        sum_small[:, bc_cols : bc_cols + dt_cols],
        summed[:taps],
        summed[taps],
        summed[taps + 2].reshape(conv_bc.shape),
        rest[:bc_cols],
        rest[bc_cols : bc_cols + heads],
        rest[bc_cols + heads : bc_cols + 2 * heads],
        rest[bc_cols + 2 * heads : bc_cols + 3 * heads],
        summed[taps + 1],
        sum_out.T,
    )


def solution(mesh):
    placed = (
        P(("dp", "tensor"), None),
        P(("dp", "tensor"), None),
        P("dp"),
        P(),
        P("dp", "tensor"),
        P("dp", "tensor"),
        P("dp", None),
        P("dp", "tensor"),
        P(None, "tensor"),
        P("tensor"),
        P(),
        P(),
        P("tensor"),
        P("tensor"),
        P("tensor"),
        P("tensor"),
        P("tensor", "dp"),
    )
    return jax.shard_map(
        body,
        mesh=mesh,
        in_specs=placed,
        out_specs=(
            P(("dp", "tensor"), None),
            P(("dp", "tensor"), None),
            P(),
            P("dp", "tensor"),
            P("dp", "tensor"),
            P("dp", None),
            P("dp", "tensor"),
            P(None, "tensor"),
            P("tensor"),
            P(),
            P(),
            P("tensor"),
            P("tensor"),
            P("tensor"),
            P("tensor"),
            P("tensor", "dp"),
        ),
        check_vma=False,
    )
```

```python
import functools

import jax
import jax.numpy as jnp
from jax import lax
from jax.experimental import pallas as pl
from jax.experimental.pallas import tpu as pltpu
from jax.sharding import PartitionSpec as P

HEADS = 32
HEAD_DIM = 64
STATE = 128
LANES = 128
MESH = pl.DeviceIdType.MESH

EPSILON = 1e-05
HIGHEST = lax.Precision.HIGHEST


def chip_at(pos, chips):
    pos = lax.rem(pos + 4 * chips, chips)
    up = (pos < chips // 2).astype(jnp.int32)
    return up * (2 * pos) + (1 - up) * (2 * (chips - 1 - pos) + 1)


def place_of(chip, chips):
    odd = lax.rem(chip, 2)
    return (1 - odd) * (chip // 2) + odd * (chips - 1 - chip // 2)


def gather_kernel(
    chips, wg, wx, wo, wb, nrm, grd, og, ox, oo, ob, on, ogr,
    ring_send, ring_recv, sib_send, sib_recv, ten_send, ten_recv, loc_sem,
):
    me = lax.axis_index("dp")
    rank = lax.axis_index("tensor")
    core = lax.rem(me, 2)
    chip = me // 2
    way = 1 - 2 * core
    pos = place_of(chip, chips)
    right = 2 * chip_at(pos + way, chips) + core
    left = 2 * chip_at(pos - way, chips) + core
    sibling = 2 * chip + 1 - core
    other = 1 - rank
    barrier = pltpu.get_barrier_semaphore()
    for target in ((right, rank), (left, rank), (sibling, rank), (me, other)):
        pl.semaphore_signal(barrier, inc=1, device_id=target, device_id_type=MESH)
    pl.semaphore_wait(barrier, 4)
    ins = (wg, wx, wo, wb)
    outs = (og, ox, oo, ob)

    def owned(step, which_core):
        turn = 1 - 2 * which_core
        return 2 * chip_at(pos - step * turn, chips) + which_core

    def ring(step, piece, arriving=False):
        slot = owned(step + 1 if arriving else step, core)
        dst = outs[piece].at[slot]
        src = ins[piece] if (step == 0 and not arriving) else dst
        return pltpu.make_async_remote_copy(
            src_ref=src, dst_ref=dst, send_sem=ring_send.at[step, piece],
            recv_sem=ring_recv.at[step, piece], device_id=(right, rank), device_id_type=MESH,
        )

    def side(step, piece, arriving=False):
        slot = owned(step, 1 - core if arriving else core)
        dst = outs[piece].at[slot]
        src = ins[piece] if (step == 0 and not arriving) else dst
        return pltpu.make_async_remote_copy(
            src_ref=src, dst_ref=dst, send_sem=sib_send.at[step, piece],
            recv_sem=sib_recv.at[step, piece], device_id=(sibling, rank), device_id_type=MESH,
        )

    def over(which, arriving=False):
        slot = other if arriving else rank
        src = (nrm, grd)[which]
        return pltpu.make_async_remote_copy(
            src_ref=src, dst_ref=(on, ogr)[which].at[slot], send_sem=ten_send.at[which],
            recv_sem=ten_recv.at[which], device_id=(me, other), device_id_type=MESH,
        )

    for piece in range(4):
        ring(0, piece).start()
    for which in range(2):
        over(which).start()
    for piece in range(4):
        side(0, piece).start()
    local = [pltpu.make_async_copy(ins[p], outs[p].at[me], loc_sem.at[p]) for p in range(4)]
    local += [
        pltpu.make_async_copy((nrm, grd)[w], (on, ogr)[w].at[rank], loc_sem.at[4 + w])
        for w in range(2)
    ]
    for copy in local:
        copy.start()
    for step in range(1, chips):
        for piece in range(4):
            ring(step - 1, piece, True).wait_recv()
            if step < chips - 1:
                ring(step, piece).start()
            side(step, piece).start()
    for copy in local:
        copy.wait()
    for which in range(2):
        over(which).wait_send()
        over(which, True).wait_recv()
    for step in range(chips):
        for piece in range(4):
            if step < chips - 1:
                ring(step, piece).wait_send()
            side(step, piece).wait_send()
            side(step, piece, True).wait_recv()


def gather_all(wg, wx, wo, wb, nrm, grd):
    count = lax.axis_size("dp")
    chips = count // 2
    anywhere = pl.BlockSpec(memory_space=pl.ANY)
    dma = pltpu.SemaphoreType.DMA
    outs = [jax.ShapeDtypeStruct((count,) + a.shape, a.dtype) for a in (wg, wx, wo, wb)]
    outs += [jax.ShapeDtypeStruct((2,) + a.shape, a.dtype) for a in (nrm, grd)]
    res = pl.pallas_call(
        functools.partial(gather_kernel, chips),
        out_shape=outs,
        in_specs=[anywhere] * 6,
        out_specs=[anywhere] * 6,
        scratch_shapes=[
            dma((chips - 1, 4)), dma((chips - 1, 4)), dma((chips, 4)), dma((chips, 4)),
            dma((2,)), dma((2,)), dma((6,)),
        ],
        compiler_params=pltpu.CompilerParams(collective_id=0, has_side_effects=True),
        name="gather_weights",
    )(wg, wx, wo, wb, nrm, grd)
    return [r.reshape(r.shape[0] * r.shape[1], r.shape[2]) for r in res]


def reduce_kernel(
    chips, stages, gg, gx, go, gb, small, mine, theirs, scaled, og, ox, oo, ob, osmall, onorm,
    sg, sx, so, sb, tg, tx, to, tb, rg, rx, ro, rb, acc, got, landed,
    sib_send, sib_recv, ring_send, ring_recv, fly_send, fly_recv, ten_send, ten_recv,
):
    me = lax.axis_index("dp")
    rank = lax.axis_index("tensor")
    core = lax.rem(me, 2)
    chip = me // 2
    way = 1 - 2 * core
    pos = place_of(chip, chips)
    right = 2 * chip_at(pos + way, chips) + core
    left = 2 * chip_at(pos - way, chips) + core
    sibling = 2 * chip + 1 - core
    other = 1 - rank

    def partner(stage):
        if stage == stages:
            return (me, other)
        bit = 1 << stage
        return (me + bit - 2 * bit * lax.rem(me // bit, 2), rank)

    barrier = pltpu.get_barrier_semaphore()
    targets = [(right, rank), (left, rank)] + [partner(s) for s in range(stages + 1)]
    for target in targets:
        pl.semaphore_signal(barrier, inc=1, device_id=target, device_id_type=MESH)
    pl.semaphore_wait(barrier, len(targets))
    ins = (gg, gx, go, gb)
    sibs = (sg, sx, so, sb)
    sends = (tg, tx, to, tb)
    gots = (rg, rx, ro, rb)
    outs = (og, ox, oo, ob)

    def target_chip(step, which_core):
        turn = 1 - 2 * which_core
        return chip_at(pos - turn * (1 + step), chips)

    def side(step, piece):
        src = ins[piece].at[2 * target_chip(step, 1 - core) + 1 - core]
        return pltpu.make_async_remote_copy(
            src_ref=src, dst_ref=sibs[piece].at[step], send_sem=sib_send.at[step, piece],
            recv_sem=sib_recv.at[step, piece], device_id=(sibling, rank), device_id_type=MESH,
        )

    def ring(step, piece):
        return pltpu.make_async_remote_copy(
            src_ref=sends[piece].at[step], dst_ref=gots[piece].at[step],
            send_sem=ring_send.at[step, piece], recv_sem=ring_recv.at[step, piece],
            device_id=(right, rank), device_id_type=MESH,
        )

    def fly(stage):
        rows = pl.ds(8, 8) if stage == stages else pl.ds(0, 16)
        return pltpu.make_async_remote_copy(
            src_ref=acc.at[stage, rows], dst_ref=got.at[stage, rows],
            send_sem=fly_send.at[stage], recv_sem=fly_recv.at[stage],
            device_id=partner(stage), device_id_type=MESH,
        )

    def fly_end(stage):
        fly(stage).wait_recv()
        if stage == stages:
            osmall[pl.ds(0, 8), :] = acc[stage, pl.ds(0, 8), :]
            osmall[pl.ds(8, 8), :] = acc[stage, pl.ds(8, 8), :] + got[stage, pl.ds(8, 8), :]
        else:
            acc[stage + 1] = acc[stage] + got[stage]

    for piece in range(4):
        side(0, piece).start()
    across = pltpu.make_async_remote_copy(
        src_ref=theirs, dst_ref=landed, send_sem=ten_send.at[0], recv_sem=ten_recv.at[0],
        device_id=(me, other), device_id_type=MESH,
    )
    across.start()
    for step in range(1, chips):
        for piece in range(4):
            side(step, piece).start()
    for step in range(chips):
        own = 2 * target_chip(step, core) + core
        for piece in range(4):
            side(step, piece).wait_recv()
            total = ins[piece][own].astype(jnp.float32) + sibs[piece][step].astype(jnp.float32)
            if step > 0:
                ring(step - 1, piece).wait_recv()
                total = total + gots[piece][step - 1].astype(jnp.float32)
            if step < chips - 1:
                sends[piece][step] = total.astype(jnp.bfloat16)
                ring(step, piece).start()
            else:
                outs[piece][...] = total
        if step == 0:
            across.wait_recv()
            grad_normed = mine[...] + landed[...].astype(jnp.float32)
            onorm[...] = grad_normed
            acc[0] = small[...]
            acc[0, pl.ds(8, 1), :] = jnp.sum(scaled[...] * grad_normed, axis=0, keepdims=True)
            fly(0).start()
        elif step <= stages + 1:
            fly_end(step - 1)
            if step <= stages:
                fly(step).start()
    for stage in range(chips - 1, stages + 1):
        fly_end(stage)
        if stage < stages:
            fly(stage + 1).start()
    for step in range(chips):
        for piece in range(4):
            side(step, piece).wait_send()
            if step < chips - 1:
                ring(step, piece).wait_send()
    for stage in range(stages + 1):
        fly(stage).wait_send()
    across.wait_send()


def reduce_all(gg, gx, go, gb, small, mine, theirs, scaled):
    count = lax.axis_size("dp")
    chips = count // 2
    stages = count.bit_length() - 1
    vmem = pl.BlockSpec(memory_space=pltpu.VMEM)
    dma = pltpu.SemaphoreType.DMA
    parts = [g.reshape(count, g.shape[0] // count, g.shape[1]) for g in (gg, gx, go, gb)]
    outs = [jax.ShapeDtypeStruct(p.shape[1:], jnp.float32) for p in parts]
    outs.append(jax.ShapeDtypeStruct(small.shape, jnp.float32))
    outs.append(jax.ShapeDtypeStruct(mine.shape, jnp.float32))
    bufs = [pltpu.VMEM((chips,) + p.shape[1:], jnp.bfloat16) for p in parts]
    slots = [pltpu.VMEM((chips - 1,) + p.shape[1:], jnp.bfloat16) for p in parts]
    return pl.pallas_call(
        functools.partial(reduce_kernel, chips, stages),
        out_shape=outs,
        in_specs=[vmem] * 8,
        out_specs=[vmem] * 6,
        scratch_shapes=bufs + slots + slots + [
            pltpu.VMEM((stages + 1,) + small.shape, jnp.float32),
            pltpu.VMEM((stages + 1,) + small.shape, jnp.float32),
            pltpu.VMEM(theirs.shape, theirs.dtype),
            dma((chips, 4)), dma((chips, 4)), dma((chips - 1, 4)), dma((chips - 1, 4)),
            dma((stages + 1,)), dma((stages + 1,)), dma((1,)), dma((1,)),
        ],
        compiler_params=pltpu.CompilerParams(
            collective_id=1, has_side_effects=True, vmem_limit_bytes=50 * 1024 * 1024
        ),
        name="reduce_grads",
    )(*parts, small, mine, theirs, scaled)


def swap(values):
    return lax.ppermute(values, "tensor", [(0, 1), (1, 0)])


def pair_sum(values):
    return values + swap(values)


def pair_scatter(values, rank):
    rows = values.shape[0] // 2
    halves = values.reshape(2, rows, values.shape[1])
    mine = lax.dynamic_index_in_dim(halves, rank, 0, keepdims=False)
    theirs = lax.dynamic_index_in_dim(halves, 1 - rank, 0, keepdims=False)
    return mine + swap(theirs.astype(jnp.bfloat16)).astype(jnp.float32)


def causal_conv(values, kernel, offsets):
    taps_count = kernel.shape[0]
    length_rows = values.shape[0]
    padded = jnp.concatenate(
        [jnp.zeros((taps_count - 1, values.shape[1]), values.dtype), values], axis=0
    )
    summed = offsets[None, :] + jnp.zeros_like(values)
    for tap_index in range(taps_count):
        summed = summed + kernel[tap_index][None, :] * padded[tap_index : tap_index + length_rows]
    return summed


def mix_bc(bc_raw, conv_bc, conv_bc_bias):
    return jax.nn.silu(causal_conv(bc_raw, conv_bc, conv_bc_bias))


ROWS = (((0,), (0,)), ((), ()))
COLS = (((1,), (1,)), ((), ()))
PLAIN = (((1,), (0,)), ((), ()))


def halves_of(values):
    high = values.astype(jnp.bfloat16)
    return high, (values - high.astype(jnp.float32)).astype(jnp.bfloat16)


def split_dot(left, right, dims):
    def one(x, y):
        return lax.dot_general(x, y, dims, preferred_element_type=jnp.float32)

    return one(left[0], right[0]) + (one(left[0], right[1]) + one(left[1], right[0]))


def shifted(values, count, rows):
    if count == 0:
        return values
    size = values.shape[0]
    rolled = pltpu.roll(values, count % size, 0)
    keep = rows >= count if count > 0 else rows < size + count
    return jnp.where(keep, rolled, 0.0)


def pick_column(values, index, lanes):
    return jnp.sum(jnp.where(lanes == index, values, 0.0), axis=1, keepdims=True)


def conv_parts(x_ref, par_ref, rows, taps):
    x_raw = x_ref[...]
    moved = [shifted(x_raw, taps - 1 - j, rows) for j in range(taps)]
    summed = par_ref[pl.ds(taps, 1), :] + jnp.zeros_like(x_raw)
    for j in range(taps):
        summed = summed + par_ref[pl.ds(j, 1), :] * moved[j]
    sig = 1.0 / (1.0 + jnp.exp(-summed))
    return moved, summed, sig


def head_decay(log_ref, log_t_ref, head, lanes, causal):
    column = pick_column(log_ref[...], head, lanes)
    gaps = column - log_t_ref[pl.ds(head, 1), :]
    return jnp.where(causal, jnp.exp(jnp.where(causal, gaps, 0.0)), 0.0)


def scan_setup(bc_ref, cross_ref):
    @pl.when(pl.program_id(0) == 0)
    def _():
        cross_ref[...] = lax.dot_general(
            bc_ref[:, STATE:], bc_ref[:, :STATE], COLS,
            precision=HIGHEST, preferred_element_type=jnp.float32,
        )

    size = cross_ref.shape[0]
    rows = lax.broadcasted_iota(jnp.int32, (size, LANES), 0)
    lanes = lax.broadcasted_iota(jnp.int32, (size, LANES), 1)
    wide_rows = lax.broadcasted_iota(jnp.int32, (size, size), 0)
    wide_cols = lax.broadcasted_iota(jnp.int32, (size, size), 1)
    return rows, lanes, wide_rows, wide_cols


def scan_kernel(taps, x_ref, bc_ref, par_ref, dt_ref, log_ref, log_t_ref, y_ref, cross_ref):
    rows, lanes, wide_rows, wide_cols = scan_setup(bc_ref, cross_ref)
    causal = wide_rows >= wide_cols
    base = 2 * pl.program_id(0)
    left = lanes < HEAD_DIM
    _, summed, sig = conv_parts(x_ref, par_ref, rows, taps)
    x_vals = summed * sig
    dt_all = dt_ref[...]
    dt_pair = jnp.where(
        left, pick_column(dt_all, base, lanes), pick_column(dt_all, base + 1, lanes)
    )
    weighted = halves_of(x_vals * dt_pair)
    parts = []
    for k in range(2):
        mixing = cross_ref[...] * head_decay(log_ref, log_t_ref, base + k, lanes, causal)
        parts.append(split_dot(halves_of(mixing), weighted, PLAIN))
    y_ref[...] = jnp.where(left, parts[0], parts[1]) + par_ref[pl.ds(taps + 1, 1), :] * x_vals


def back_kernel(
    taps, x_ref, bc_ref, par_ref, dt_ref, log_ref, log_t_ref, gy_ref,
    gx_ref, gbc_ref, gpar_ref, gdt_ref, grow_ref, gcol_ref, cross_ref, gcross_ref,
):
    step = pl.program_id(0)

    @pl.when(step == 0)
    def _():
        gcross_ref[...] = jnp.zeros_like(gcross_ref)
        gdt_ref[...] = jnp.zeros_like(gdt_ref)
        grow_ref[...] = jnp.zeros_like(grow_ref)

    rows, lanes, wide_rows, wide_cols = scan_setup(bc_ref, cross_ref)
    causal = wide_rows >= wide_cols
    strict = wide_rows > wide_cols
    base = 2 * step
    left = lanes < HEAD_DIM
    moved, summed, sig = conv_parts(x_ref, par_ref, rows, taps)
    x_vals = summed * sig
    dt_all = dt_ref[...]
    dt_pair = jnp.where(
        left, pick_column(dt_all, base, lanes), pick_column(dt_all, base + 1, lanes)
    )
    weighted = halves_of(x_vals * dt_pair)
    grad_y = gy_ref[...]
    parts = []
    for k in range(2):
        own = left if k == 0 else jnp.logical_not(left)
        grad_own = halves_of(jnp.where(own, grad_y, 0.0))
        decay = head_decay(log_ref, log_t_ref, base + k, lanes, causal)
        grad_decayed = split_dot(grad_own, weighted, COLS) * decay
        gcross_ref[...] += grad_decayed
        mixing = cross_ref[...] * decay
        parts.append(split_dot(halves_of(mixing), grad_own, ROWS))
        flow = jnp.where(strict, grad_decayed * cross_ref[...], 0.0)
        grow_ref[...] += jnp.where(lanes == base + k, jnp.sum(flow, axis=1, keepdims=True), 0.0)
        gcol_ref[pl.ds(base + k, 1), :] = jnp.sum(flow, axis=0, keepdims=True)
    grad_w = parts[0] + parts[1]
    through = grad_w * x_vals
    for k in range(2):
        own = left if k == 0 else jnp.logical_not(left)
        total = jnp.sum(jnp.where(own, through, 0.0), axis=1, keepdims=True)
        gdt_ref[...] += jnp.where(lanes == base + k, total, 0.0)
    grad_x = grad_w * dt_pair + par_ref[pl.ds(taps + 1, 1), :] * grad_y
    grad_sum = grad_x * sig * (1.0 + summed * (1.0 - sig))
    back = jnp.zeros_like(grad_sum)
    for j in range(taps):
        back = back + par_ref[pl.ds(j, 1), :] * shifted(grad_sum, j + 1 - taps, rows)
        gpar_ref[pl.ds(j, 1), :] = jnp.sum(grad_sum * moved[j], axis=0, keepdims=True)
    gpar_ref[pl.ds(taps, 1), :] = jnp.sum(grad_sum, axis=0, keepdims=True)
    gpar_ref[pl.ds(taps + 1, 1), :] = jnp.sum(grad_y * x_vals, axis=0, keepdims=True)
    gpar_ref[pl.ds(taps + 2, 2), :] = jnp.zeros((2, LANES), jnp.float32)
    gx_ref[...] = back.astype(jnp.bfloat16)

    @pl.when(step == pl.num_programs(0) - 1)
    def _():
        pair = gcross_ref[...]
        gbc_ref[:, STATE:] = lax.dot_general(
            pair, bc_ref[:, :STATE], PLAIN, precision=HIGHEST, preferred_element_type=jnp.float32
        )
        gbc_ref[:, :STATE] = lax.dot_general(
            pair, bc_ref[:, STATE:], ROWS, precision=HIGHEST, preferred_element_type=jnp.float32
        )


def mixer_call(taps, backward, x_raw, *args):
    size, width = x_raw.shape
    f32 = jnp.float32
    block = pl.BlockSpec((size, LANES), lambda i: (0, i))
    narrow = pl.BlockSpec((8, LANES), lambda i: (0, i))

    def whole(shape):
        return pl.BlockSpec(shape, lambda i: (0, 0))

    bc_vals, params, dt_pad, log_pad, log_t = args[:5]
    in_specs = [block, whole(bc_vals.shape), narrow] + [whole(a.shape) for a in args[2:5]]
    square = pltpu.VMEM((size, size), f32)
    if backward:
        in_specs.append(block)
        out_shape = [
            jax.ShapeDtypeStruct((size, width), jnp.bfloat16),
            jax.ShapeDtypeStruct(bc_vals.shape, f32),
            jax.ShapeDtypeStruct(params.shape, f32),
            jax.ShapeDtypeStruct(dt_pad.shape, f32),
            jax.ShapeDtypeStruct(dt_pad.shape, f32),
            jax.ShapeDtypeStruct(log_t.shape, f32),
        ]
        out_specs = [block, whole(bc_vals.shape), narrow] + [whole(o.shape) for o in out_shape[3:]]
    else:
        out_shape = jax.ShapeDtypeStruct((size, width), f32)
        out_specs = block
    return pl.pallas_call(
        functools.partial(back_kernel if backward else scan_kernel, taps),
        grid=(width // LANES,),
        out_shape=out_shape,
        in_specs=in_specs,
        out_specs=out_specs,
        scratch_shapes=[square, square] if backward else [square],
        compiler_params=pltpu.CompilerParams(vmem_limit_bytes=40 * 1024 * 1024),
        cost_estimate=pl.CostEstimate(
            flops=(3 if backward else 1) * 6 * size * size * width,
            bytes_accessed=8 * size * width, transcendentals=size * size * width // HEAD_DIM,
        ),
        name="mixer_back" if backward else "mixer_scan",
    )(x_raw, *args)


def times_right(left, right):
    return jnp.dot(left, right, preferred_element_type=jnp.float32)


def times_back(left, right):
    return lax.dot_general(
        left, right, (((1,), (1,)), ((), ())), preferred_element_type=jnp.float32
    )


def over_rows(left, right):
    return lax.dot_general(
        left, right, (((0,), (0,)), ((), ())), preferred_element_type=jnp.float32
    )


def body(
    hidden,
    cotangent,
    lengths,
    norm_gain,
    w_gate,
    w_x,
    w_bc,
    w_dt,
    conv_x,
    conv_x_bias,
    conv_bc,
    conv_bc_bias,
    dt_bias,
    a_log,
    d_skip,
    gated_gain,
    w_out,
):
    own_rows, model_width = hidden.shape
    rank = lax.axis_index("tensor")
    inner_width = HEADS * HEAD_DIM
    bc_cols = w_bc.shape[1]
    dt_cols = w_dt.shape[1]
    fill = -(bc_cols + dt_cols) % LANES
    hidden_vals = hidden.astype(jnp.float32)
    row_scale = lax.rsqrt(jnp.mean(hidden_vals * hidden_vals, axis=1, keepdims=True) + EPSILON)
    normed_own = (hidden_vals * row_scale * norm_gain[None, :]).astype(jnp.bfloat16)
    positions = rank * own_rows + jnp.arange(own_rows, dtype=jnp.int32)
    live_rows = (positions < lengths[0]).astype(jnp.float32)[:, None]
    cot_vals = cotangent.astype(jnp.float32)
    grad_branch = (live_rows * cot_vals).astype(jnp.bfloat16)
    w_small = jnp.concatenate([w_bc, w_dt, jnp.zeros((w_bc.shape[0], fill), w_bc.dtype)], axis=1)
    full_gate, full_x, full_out, full_small, normed, grad_full = gather_all(
        w_gate, w_x, w_out.T, w_small, normed_own, grad_branch
    )
    gate_raw = times_right(normed, full_gate)
    x_raw = times_right(normed, full_x)
    small_raw = times_right(normed, full_small)
    bc_raw = small_raw[:, :bc_cols]
    dt_raw = small_raw[:, bc_cols : bc_cols + dt_cols]
    bc_vals, bc_pull = jax.vjp(mix_bc, bc_raw, conv_bc, conv_bc_bias)
    heads = dt_cols
    taps = conv_x.shape[0]
    dt_in = dt_raw + dt_bias[None, :]
    dt_vals = jax.nn.softplus(dt_in)
    rates = -jnp.exp(a_log)
    size = dt_vals.shape[0]
    lower = jnp.tril(jnp.ones((size, size), jnp.float32))
    log_decay = jnp.dot(lower, dt_vals * rates[None, :], precision=HIGHEST)
    wide = ((0, 0), (0, LANES - heads))
    params = jnp.concatenate(
        [
            conv_x,
            conv_x_bias[None],
            jnp.repeat(d_skip, HEAD_DIM)[None],
            jnp.zeros((2, conv_x.shape[1]), jnp.float32),
        ],
        axis=0,
    )
    mix_args = (bc_vals, params, jnp.pad(dt_vals, wide), jnp.pad(log_decay, wide), log_decay.T)
    mixer_out = mixer_call(taps, False, x_raw, *mix_args)
    gate_act = jax.nn.silu(gate_raw)
    gated_vals = mixer_out * gate_act
    grad_y = times_right(grad_full, full_out)
    weighted_grad = grad_y * gated_gain[None, :]
    row_sums = pair_sum(
        jnp.stack(
            [jnp.sum(gated_vals * gated_vals, axis=1), jnp.sum(gated_vals * weighted_grad, axis=1)]
        )
    )
    gate_scale = lax.rsqrt(row_sums[0] / inner_width + EPSILON)[:, None]
    cross_sum = row_sums[1]
    normed_y = (gated_vals * gate_scale * gated_gain[None, :]).astype(jnp.bfloat16)
    branch_own = pair_scatter(times_back(normed_y, full_out), rank)
    output = (hidden_vals + live_rows * branch_own).astype(jnp.bfloat16)
    grad_w_out = over_rows(grad_full, normed_y).astype(jnp.bfloat16)
    grad_gated_gain = jnp.sum(grad_y * gated_vals * gate_scale, axis=0)
    grad_gated = (
        gate_scale * weighted_grad - gated_vals * gate_scale**3 * (cross_sum / inner_width)[:, None]
    )
    gate_sigmoid = jax.nn.sigmoid(gate_raw)
    grad_mixer = grad_gated * gate_act
    grad_gate = (
        grad_gated * mixer_out * gate_sigmoid * (1.0 + gate_raw * (1.0 - gate_sigmoid))
    ).astype(jnp.bfloat16)
    grad_x, grad_bc_part, grad_params, direct, from_rows, from_cols = mixer_call(
        taps, True, x_raw, *mix_args, grad_mixer
    )
    grad_bc_f, grad_conv_bc, grad_conv_bc_bias = bc_pull(pair_sum(grad_bc_part))
    grad_log = from_rows[:, :heads] - from_cols.T
    grad_step = lax.dot_general(lower, grad_log, ROWS, precision=HIGHEST)
    grad_dt_f = (direct[:, :heads] + grad_step * rates[None, :]) * jax.nn.sigmoid(dt_in)
    grad_dt_bias = jnp.sum(grad_dt_f, axis=0)
    grad_a_log = rates * jnp.sum(grad_step * dt_vals, axis=0)
    grad_conv_x = grad_params[:taps]
    grad_conv_x_bias = grad_params[taps]
    grad_d_skip = jnp.sum(grad_params[taps + 1].reshape(heads, HEAD_DIM), axis=1)
    grad_bc = grad_bc_f.astype(jnp.bfloat16)
    grad_dt = grad_dt_f.astype(jnp.bfloat16)
    tail = jnp.zeros((grad_dt.shape[0], fill), jnp.bfloat16)
    grad_small = jnp.concatenate([grad_bc, grad_dt, tail], axis=1)
    first = (rank == 0).astype(jnp.bfloat16)
    grad_kept = jnp.concatenate([grad_bc * first, grad_dt, tail], axis=1)
    g_gate = over_rows(normed, grad_gate).astype(jnp.bfloat16)
    g_x = over_rows(normed, grad_x).astype(jnp.bfloat16)
    g_small = over_rows(normed, grad_small).astype(jnp.bfloat16)
    grad_normed = (
        times_back(grad_gate, full_gate)
        + times_back(grad_x, full_x)
        + times_back(grad_kept, full_small)
    )
    halves = grad_normed.reshape(2, own_rows, model_width)
    mine = lax.dynamic_index_in_dim(halves, rank, 0, keepdims=False)
    theirs = lax.dynamic_index_in_dim(halves, 1 - rank, 0, keepdims=False).astype(jnp.bfloat16)
    mixed = jnp.concatenate([grad_conv_bc_bias, grad_dt_bias, grad_a_log, grad_d_skip])
    small = jnp.concatenate(
        [
            grad_conv_x,
            grad_conv_x_bias[None],
            grad_gated_gain[None],
            grad_conv_bc.reshape(1, -1),
            jnp.pad(mixed, (0, model_width - mixed.shape[0]))[None],
            jnp.zeros((8, model_width), jnp.float32),
        ],
        axis=0,
    )
    sum_gate, sum_x, sum_out, sum_small, summed, grad_normed_own = reduce_all(
        g_gate, g_x, grad_w_out, g_small, small, mine, theirs, hidden_vals * row_scale
    )
    weighted_in = grad_normed_own * norm_gain[None, :]
    inner_sum = jnp.sum(hidden_vals * weighted_in, axis=1, keepdims=True)
    grad_hidden = row_scale * weighted_in - hidden_vals * row_scale**3 * inner_sum / model_width
    d_hidden = (cot_vals + grad_hidden).astype(jnp.bfloat16)
    rest = summed[taps + 3]
    return (
        output,
        d_hidden,
        summed[8],
        sum_gate,
        sum_x,
        sum_small[:, :bc_cols],
        sum_small[:, bc_cols : bc_cols + dt_cols],
        summed[:taps],
        summed[taps],
        summed[taps + 2].reshape(conv_bc.shape),
        rest[:bc_cols],
        rest[bc_cols : bc_cols + heads],
        rest[bc_cols + heads : bc_cols + 2 * heads],
        rest[bc_cols + 2 * heads : bc_cols + 3 * heads],
        summed[taps + 1],
        sum_out.T,
    )


def solution(mesh):
    placed = (
        P(("dp", "tensor"), None),
        P(("dp", "tensor"), None),
        P("dp"),
        P(),
        P("dp", "tensor"),
        P("dp", "tensor"),
        P("dp", None),
        P("dp", "tensor"),
        P(None, "tensor"),
        P("tensor"),
        P(),
        P(),
        P("tensor"),
        P("tensor"),
        P("tensor"),
        P("tensor"),
        P("tensor", "dp"),
    )
    return jax.shard_map(
        body,
        mesh=mesh,
        in_specs=placed,
        out_specs=(
            P(("dp", "tensor"), None),
            P(("dp", "tensor"), None),
            P(),
            P("dp", "tensor"),
            P("dp", "tensor"),
            P("dp", None),
            P("dp", "tensor"),
            P(None, "tensor"),
            P("tensor"),
            P(),
            P(),
            P("tensor"),
            P("tensor"),
            P("tensor"),
            P("tensor"),
            P("tensor", "dp"),
        ),
        check_vma=False,
    )
```
